32 devices in a mesh: sx: 4 (over y, core), sy: 8 (over z, x).
Axes of the slice: x: 2, y: 2, z: 4, core: 2. Of those that a mesh axis runs over, the one named last changes fastest.
Arguments:
- skip_features: bfloat16 [1024, 64, 128], P(('sx', 'sy')), may hold values from -6 to 6
- coarse_features: bfloat16 [256, 64, 128], P(('sx', 'sy')), may hold values from -6 to 6
- child_code: int32 [1024], P(('sx', 'sy')), may hold values from 0 to 63
- neighbours: int32 [1024, 27], P(('sx', 'sy')), may hold values from -1 to 71, as said below
- send_face: int32 [32, 4, 8], P(('sx', 'sy')), may hold values from 0 to 31, as said below
- send_corner: int32 [32, 4, 2], P(('sx', 'sy')), may hold values from 0 to 31, as said below
- live_count: int32 [32], P(('sx', 'sy')), may hold values from 8 to 32, as said below
- weight: bfloat16 [27, 128, 128], replicated, may hold values from -0.109375 to 0.109375
- conv_bias: float32 [128], replicated, may hold values from -3 to 3
- cotangent: bfloat16 [1024, 64, 128], P(('sx', 'sy')), may hold values from -6 to 6
Outputs:
- activated: bfloat16 [1024, 64, 128], P(('sx', 'sy'))
- skip_grad: bfloat16 [1024, 64, 128], P(('sx', 'sy'))
- coarse_grad: bfloat16 [256, 64, 128], P(('sx', 'sy'))
- weight_grad: float32 [27, 128, 128], replicated
- bias_grad: float32 [128], replicated
The draws below stay inside these ranges and needn't reach their ends.
Inputs may be any that keep to these rules, and one draw needn't show every extreme that they name: `live_count`: one device has all 32 slots live; slots from the count on are empty. `send_face`: slots of live bricks of the sending device, distinct within one list. `send_corner`: slots of live bricks of the sending device, distinct within one list. `neighbours`: for a live slot, entries below 32 name live slots of the same device; offset 13 names the slot itself.
All inputs are finite; a program needn't handle non-finite values.
Results may differ from the reference program's by a relative error of at most 0.0056.
Values may be sent and summed in bfloat16 or wider, within the bound.
A program may use at most 128 MiB of HBM per device.

```python
import jax
import jax.numpy as jnp
from jax import lax

C = 128
BR = 32
CAP = 8
CAPC = 2
BRP = 8
DEVS = 32
NB = 1024
N_SX = 4
N_SY = 8


def live_draw(key):
    base_key = jax.random.fold_in(key, 101)
    chosen_key = jax.random.fold_in(key, 102)
    counts = jax.random.randint(base_key, (DEVS,), BR // 4, BR // 2 + 1)
    busiest = jax.random.randint(chosen_key, (), 0, DEVS)
    return jnp.where(jnp.arange(DEVS) == busiest, BR, counts).astype(jnp.int32)


def pick_slots(key, lanes, capacity, salt):
    counts = live_draw(key)
    scores = jax.random.randint(jax.random.fold_in(key, salt), (DEVS, lanes, BR), 0, 1 << 20)
    empty_slot = jnp.arange(BR)[None, None, :] >= counts[:, None, None]
    scores = scores + jnp.where(empty_slot, 1 << 21, 0)
    ordered = jnp.argsort(scores, axis=-1, stable=True)
    return ordered[:, :, :capacity].astype(jnp.int32)


def draw_live_count(key, part):
    return live_draw(key)


def draw_send_face(key, part):
    return pick_slots(key, 4, CAP, 301)


def draw_send_corner(key, part):
    return pick_slots(key, 4, CAPC, 302)


def draw_neighbours(key, part):
    counts = live_draw(key)
    kinds = jax.random.randint(jax.random.fold_in(key, 401), (DEVS, BR, 27), 0, 12)
    local_pick = jax.random.randint(jax.random.fold_in(key, 402), (DEVS, BR, 27), 0, 1 << 20) % counts[:, None, None]
    remote_pick = BR + jax.random.randint(jax.random.fold_in(key, 403), (DEVS, BR, 27), 0, 4 * CAP + 4 * CAPC)
    chosen = jnp.where(kinds < 4, -1, jnp.where(kinds < 10, local_pick, remote_pick))
    centre = jnp.broadcast_to(jnp.arange(BR)[None, :], (DEVS, BR))
    chosen = chosen.at[:, :, 13].set(centre)
    return chosen.reshape(DEVS * BR, 27).astype(jnp.int32)


def touch_ends(entries, own_key, least, largest):
    longest = entries.shape.index(max(entries.shape))
    spots = []
    for shift in (0, 1):
        where = [jax.random.randint(jax.random.fold_in(own_key, axis), (), 0, length) for axis, length in enumerate(entries.shape)]
        where[longest] = (where[longest] + shift) % entries.shape[longest]
        spots.append(tuple(where))
    return entries.at[spots[0]].set(least).at[spots[1]].set(largest)


def level_of(own_key, dims, cuts, low, high):
    def one(axis_at, parts):
        heights = jax.random.uniform(jax.random.fold_in(jax.random.fold_in(own_key, 6), axis_at), (parts,), jnp.float32, low / len(cuts), high / len(cuts))
        return jnp.repeat(jnp.exp(heights), dims[axis_at] // parts).reshape((-1,) + (1,) * (len(dims) - axis_at - 1))

    level = one(*cuts[0])
    for cut in cuts[1:]:
        level = level * one(*cut)
    return level


def gaussian(rng, dims, scale, most, split=(), kind=jnp.bfloat16):
    level = level_of(rng, dims, split, -0.22, 0.18) if split else 1.0
    entries = jax.random.normal(rng, dims, jnp.float32) * scale * level
    return jnp.minimum(jnp.maximum(entries, -most), most).astype(kind)


def setup_inputs(seed: int = 0) -> dict:
    key_of = jax.random.split(jax.random.key(seed), 11)
    skip_features = gaussian(key_of[0], (NB, 64, C), 1.0, 6.0, ((0, 32),))
    coarse_features = gaussian(key_of[1], (DEVS * BRP, 64, C), 1.0, 6.0, ((0, 32),))
    child_code = touch_ends(jax.random.randint(key_of[2], (NB,), 0, 8 * BRP), jax.random.fold_in(key_of[2], 1), 0, (8 * BRP) - 1).astype(jnp.int32)
    neighbours = draw_neighbours(jax.random.fold_in(key_of[10], 71), 0)
    send_face = draw_send_face(jax.random.fold_in(key_of[10], 71), 0)
    send_corner = draw_send_corner(jax.random.fold_in(key_of[10], 71), 0)
    live_count = draw_live_count(jax.random.fold_in(key_of[10], 71), 0)
    weight = gaussian(key_of[7], (27, C, C), (27 * C) ** -0.5, 0.109375)
    conv_bias = gaussian(key_of[8], (C,), 0.5, 3.0, (), jnp.float32)
    cotangent = gaussian(key_of[9], (NB, 64, C), 1.0, 6.0, ((0, 32),))
    return dict(skip_features=skip_features, coarse_features=coarse_features, child_code=child_code, neighbours=neighbours, send_face=send_face, send_corner=send_corner, live_count=live_count, weight=weight, conv_bias=conv_bias, cotangent=cotangent)


SOURCE_SPANS = ((3, 4), (0, 4), (0, 1))
TARGET_SPANS = ((0, 1), (1, 5), (5, 6))


def voxel_table():
    voxel_ids = jnp.arange(64, dtype=jnp.int32)
    octant = jnp.arange(8, dtype=jnp.int32)
    coord_x = voxel_ids // 16
    coord_y = (voxel_ids // 4) % 4
    coord_z = voxel_ids % 4
    half_x = octant // 4
    half_y = (octant // 2) % 2
    half_z = octant % 2
    return ((2 * half_x[:, None] + coord_x[None, :] // 2) * 16 + (2 * half_y[:, None] + coord_y[None, :] // 2) * 4 + (2 * half_z[:, None] + coord_z[None, :] // 2)).astype(jnp.int32)


def padded_block(gathered, channels):
    brick_count = gathered.shape[0]
    shaped = gathered.reshape(brick_count, 27, 4, 4, 4, channels)
    planes = []
    for along_x in range(3):
        line_list = []
        for along_y in range(3):
            cell_list = []
            for along_z in range(3):
                offset = along_x * 9 + along_y * 3 + along_z
                span_x = SOURCE_SPANS[along_x]
                span_y = SOURCE_SPANS[along_y]
                span_z = SOURCE_SPANS[along_z]
                cell_list.append(shaped[:, offset, span_x[0]:span_x[1], span_y[0]:span_y[1], span_z[0]:span_z[1], :])
            line_list.append(jnp.concatenate(cell_list, axis=3))
        planes.append(jnp.concatenate(line_list, axis=2))
    return jnp.concatenate(planes, axis=1)


def unfold_taps(padded, channels):
    brick_count = padded.shape[0]
    tap_list = []
    for tap_x in range(3):
        for tap_y in range(3):
            for tap_z in range(3):
                tap_list.append(padded[:, tap_x:tap_x + 4, tap_y:tap_y + 4, tap_z:tap_z + 4, :])
    return jnp.concatenate(tap_list, axis=-1).reshape(brick_count * 64, 27 * channels)


def fold_taps(grad_cols, brick_count, channels):
    shaped = grad_cols.reshape(brick_count, 4, 4, 4, 27, channels)
    grad_pad = jnp.zeros((brick_count, 6, 6, 6, channels), jnp.float32)
    for tap_x in range(3):
        for tap_y in range(3):
            for tap_z in range(3):
                tap_id = tap_x * 9 + tap_y * 3 + tap_z
                grad_pad = grad_pad.at[:, tap_x:tap_x + 4, tap_y:tap_y + 4, tap_z:tap_z + 4, :].add(shaped[:, :, :, :, tap_id, :])
    pieces = []
    for along_x in range(3):
        for along_y in range(3):
            for along_z in range(3):
                target_x = TARGET_SPANS[along_x]
                target_y = TARGET_SPANS[along_y]
                target_z = TARGET_SPANS[along_z]
                span_x = SOURCE_SPANS[along_x]
                span_y = SOURCE_SPANS[along_y]
                span_z = SOURCE_SPANS[along_z]
                inner_part = grad_pad[:, target_x[0]:target_x[1], target_y[0]:target_y[1], target_z[0]:target_z[1], :]
                pieces.append(jnp.pad(inner_part, ((0, 0), (span_x[0], 4 - span_x[1]), (span_y[0], 4 - span_y[1]), (span_z[0], 4 - span_z[1]), (0, 0))))
    return jnp.stack(pieces, axis=1).reshape(brick_count, 27, 64, channels)


def reference(skip_features, coarse_features, child_code, neighbours, send_face, send_corner, live_count, weight, conv_bias, cotangent):
    devices = N_SX * N_SY
    slot_ids = jnp.arange(BR, dtype=jnp.int32)
    slot_live = slot_ids[None, :] < live_count[:, None]
    live_flat = slot_live.reshape(NB)
    owner_device = jnp.arange(NB, dtype=jnp.int32) // BR
    row_index = ((owner_device * BRP + child_code // 8)[:, None] * 64 + voxel_table()[child_code % 8]).astype(jnp.int32)
    upsampled = jnp.take(coarse_features.reshape(devices * BRP * 64, C), row_index, axis=0)
    hidden = ((skip_features.astype(jnp.float32) + upsampled.astype(jnp.float32)) * live_flat[:, None, None].astype(jnp.float32)).astype(jnp.bfloat16)
    index_x = jnp.arange(devices, dtype=jnp.int32) // N_SY
    index_y = jnp.arange(devices, dtype=jnp.int32) % N_SY

    def remote(step_x, step_y, send_lists, lane_id):
        source_x = index_x + step_x
        source_y = index_y + step_y
        inside = (source_x >= 0) & (source_x < N_SX) & (source_y >= 0) & (source_y < N_SY)
        source = (jnp.clip(source_x, 0, N_SX - 1) * N_SY + jnp.clip(source_y, 0, N_SY - 1)).astype(jnp.int32)
        brick_ids = source[:, None] * BR + send_lists[source, lane_id]
        return jnp.where(inside[:, None], brick_ids, -1).astype(jnp.int32)

    table_ids = jnp.concatenate([
        jnp.arange(devices, dtype=jnp.int32)[:, None] * BR + slot_ids[None, :],
        remote(-1, 0, send_face, 0), remote(1, 0, send_face, 1),
        remote(0, -1, send_face, 2), remote(0, 1, send_face, 3),
        remote(-1, -1, send_corner, 0), remote(-1, 1, send_corner, 1),
        remote(1, -1, send_corner, 2), remote(1, 1, send_corner, 3)], axis=1).astype(jnp.int32)
    local_ids = neighbours.reshape(devices, BR * 27)
    global_ids = jnp.take_along_axis(table_ids, jnp.maximum(local_ids, 0).astype(jnp.int32), axis=1)
    global_ids = jnp.where((local_ids < 0) | (global_ids < 0), NB, global_ids).astype(jnp.int32).reshape(devices, BR, 27)
    brick_table = jnp.concatenate([hidden, jnp.zeros((1, 64, C), jnp.bfloat16)], axis=0)
    flat_weight = weight.reshape(27 * C, C)

    def device_step(state_now, inputs):
        grad_hidden, weight_sum, bias_sum = state_now
        brick_ids, upstream, keep_slots = inputs
        gathered = jnp.take(brick_table, brick_ids, axis=0)
        columns = unfold_taps(padded_block(gathered, C), C)
        pre_act = jnp.dot(columns, flat_weight, preferred_element_type=jnp.float32) + conv_bias
        keep_rows = jnp.repeat(keep_slots.astype(jnp.float32), 64)[:, None]
        sigmoid_value = jax.nn.sigmoid(pre_act)
        result = (pre_act * sigmoid_value * keep_rows).astype(jnp.bfloat16)
        grad_pre = (upstream.reshape(BR * 64, C).astype(jnp.float32) * sigmoid_value * (1.0 + pre_act * (1.0 - sigmoid_value)) * keep_rows).astype(jnp.bfloat16)
        weight_sum = weight_sum + lax.dot_general(columns, grad_pre, (((0,), (0,)), ((), ())), preferred_element_type=jnp.float32)
        bias_sum = bias_sum + jnp.sum(grad_pre.astype(jnp.float32), axis=0)
        grad_cols = lax.dot_general(grad_pre, flat_weight, (((1,), (1,)), ((), ())), preferred_element_type=jnp.float32)
        pieces = fold_taps(grad_cols, BR, C)
        grad_hidden = grad_hidden.at[brick_ids.reshape(-1)].add(pieces.reshape(-1, 64, C))
        return (grad_hidden, weight_sum, bias_sum), result.reshape(BR, 64, C)

    initial = (jnp.zeros((NB + 1, 64, C), jnp.float32), jnp.zeros((27 * C, C), jnp.float32), jnp.zeros((C,), jnp.float32))
    final_state, results = lax.scan(device_step, initial, (global_ids, cotangent.reshape(devices, BR, 64, C), slot_live))
    grad_hidden, weight_sum, bias_sum = final_state
    grad_hidden = grad_hidden[:NB]
    coarse_sum = jnp.zeros((devices * BRP * 64, C), jnp.float32).at[row_index.reshape(-1)].add(grad_hidden.reshape(-1, C))
    return (results.reshape(NB, 64, C), grad_hidden.astype(jnp.bfloat16), coarse_sum.reshape(devices * BRP, 64, C).astype(jnp.bfloat16), weight_sum.reshape(27, C, C), bias_sum)
```

```python
import functools

import jax
import jax.numpy as jnp
from jax import lax
from jax.experimental import pallas as pl
from jax.experimental.pallas import tpu as pltpu
from jax.sharding import PartitionSpec as P

F32 = jnp.float32
BF16 = jnp.bfloat16
C = 128
STEPS = ((1, 0), (-1, 0), (0, 1), (0, -1), (1, 1), (1, -1), (-1, 1), (-1, -1))


def sources():
    def along(s):
        out = [(1, s + 1)]
        if s == 0:
            out.append((2, 5))
        if s == 3:
            out.append((0, 0))
        return out

    table = {}
    for x in range(4):
        for y in range(4):
            for z in range(4):
                places = []
                for a, px in along(x):
                    for b, py in along(y):
                        for c, pz in along(z):
                            o = 9 * a + 3 * b + c
                            if o != 13:
                                places.append((o, px, py, pz))
                table[16 * x + 4 * y + z] = places
    return table


def iota(shape, dim):
    return lax.broadcasted_iota(jnp.int32, shape, dim)


def one_hot(cond):
    return cond.astype(F32).astype(BF16)


def dot(a, b, dims=((1,), (0,))):
    return lax.dot_general(a, b, (dims, ((), ())), preferred_element_type=F32)


def hidden_kernel(skip, coarse, child, live, face_idx, corner_idx, hidden, faces, corners):
    bricks = skip.shape[1]
    parents = coarse.shape[1] // 8
    col = iota((bricks, 8 * parents), 1)
    pick = one_hot(child[...] == (col % parents) * 8 + col // parents)
    keep = (iota((bricks, C), 0) < live[0]).astype(F32)
    for h in range(8):
        up = dot(pick, coarse[h])
        for i in range(8):
            x, y, z = 2 * (h // 4) + i // 4, 2 * (h // 2 % 2) + i // 2 % 2, 2 * (h % 2) + i % 2
            v = 16 * x + 4 * y + z
            hidden[v] = ((skip[v].astype(F32) + up) * keep).astype(BF16)
    sel = one_hot(face_idx[...] == iota((64, 2 * bricks), 1))
    for g in range(32):
        out = dot(sel, hidden[2 * g : 2 * g + 2].reshape(2 * bricks, C)).astype(BF16)
        for e in range(4):
            faces[e, g] = out[16 * e : 16 * e + 16]
    sel = one_hot(corner_idx[...] == iota((64, 8 * bricks), 1))
    for g in range(8):
        out = dot(sel, hidden[8 * g : 8 * g + 8].reshape(8 * bricks, C)).astype(BF16)
        for e in range(4):
            corners[e, g] = out[16 * e : 16 * e + 16]


def forward_kernel(hidden, faces, corners, nb, live, weight, bias, cot, act, grad, dwt, db,
                   table, pad, hot, cols):
    hot[...] = one_hot(nb[...] == iota(hot.shape, 1))
    table[:, 0:32] = hidden[...]
    for g in range(32):
        parts = [faces[e, g].astype(F32) for e in range(4)]
        for i in range(2):
            table[2 * g + i, 32:64] = jnp.concatenate(
                [p[8 * i : 8 * i + 8] for p in parts], 0).astype(BF16)
    row = iota((128, 64), 0)
    r = row % 16
    key = jnp.where(r < 8, (r // 2) * 16 + (row // 16) * 2 + r % 2, -1)
    spread = one_hot(key == iota((128, 64), 1))
    for g in range(8):
        got = jnp.concatenate([corners[e, g] for e in range(4)], 0)
        table[8 * g : 8 * g + 8, 64:80] = dot(spread, got).astype(BF16).reshape(8, 16, C)
    for x in range(4):
        pad[x + 1, 1:5, 1:5] = hidden[16 * x : 16 * x + 16].reshape(4, 4, 32, C)
    for v, places in sources().items():
        if places:
            stack = jnp.concatenate([hot[32 * o : 32 * o + 32] for o, *_ in places], 0)
            out = dot(stack, table[v]).astype(BF16)
            for i, (_, px, py, pz) in enumerate(places):
                pad[px, py, pz] = out[32 * i : 32 * i + 32]
    dwt[...] = jnp.zeros_like(dwt)
    db[...] = jnp.zeros_like(db)
    keep = (iota((512, C), 0) % 32 < live[0]).astype(F32)

    def step(x, _):
        for t in range(27):
            tx, ty, tz = t // 9, t // 3 % 3, t % 3
            cols[:, C * t : C * t + C] = pad[x + tx, ty : ty + 4, tz : tz + 4].reshape(512, C)
        pre = dot(cols[...], weight[...]) + bias[...]
        sg = 1.0 / (1.0 + jnp.exp(-pre))
        act[pl.ds(16 * x, 16)] = (pre * sg * keep).astype(BF16).reshape(16, 32, C)
        up = cot[pl.ds(16 * x, 16)].reshape(512, C).astype(F32)
        g = (up * sg * (1.0 + pre * (1.0 - sg)) * keep).astype(BF16)
        grad[pl.ds(16 * x, 16)] = g.reshape(16, 32, C)
        g32 = g.astype(F32)
        db[...] += jnp.sum(g32.reshape(64, 8, C), 0)
        dwt[...] += dot(g32.T.astype(BF16), cols[...])
        return 0

    lax.fori_loop(0, 4, step, 0)


def backward_kernel(grad, nb, weight, own, faces, corners, gp, hot, halo):
    hot[...] = one_hot(nb[...] == iota(hot.shape, 1))
    gp[...] = jnp.zeros_like(gp)

    def step(x, _):
        g = grad[pl.ds(16 * x, 16)].reshape(512, C)
        for t in range(27):
            tx, ty, tz = t // 9, t // 3 % 3, t % 3
            out = dot(g, weight[t], ((1,), (1,)))
            gp[x + tx, ty : ty + 4, tz : tz + 4] += out.reshape(4, 4, 32, C)
        return 0

    lax.fori_loop(0, 4, step, 0)
    for v, places in sources().items():
        mid = gp[v // 16 + 1, v // 4 % 4 + 1, v % 4 + 1]
        if places:
            stack = jnp.concatenate([hot[32 * o : 32 * o + 32] for o, *_ in places], 0)
            vals = jnp.concatenate([gp[a, b, c] for _, a, b, c in places], 0).astype(BF16)
            out = dot(stack, vals, ((0,), (0,)))
            own[v] = mid + out[0:32]
            halo[v] = out[32:72]
        else:
            own[v] = mid
            halo[v] = jnp.zeros((40, C), F32)
    for g in range(32):
        for e in range(4):
            faces[e, g] = halo[2 * g : 2 * g + 2, 8 * e : 8 * e + 8].reshape(16, C).astype(BF16)
    row = iota((64, 64), 0)
    key = (row % 16 // 2) * 8 + (row // 16) * 2 + row % 2
    pack = one_hot(key == iota((64, 64), 1))
    for g in range(8):
        part = halo[8 * g : 8 * g + 8, 32:40].reshape(64, C).astype(BF16)
        out = dot(pack, part).astype(BF16)
        for e in range(4):
            corners[e, g] = out[16 * e : 16 * e + 16]


def combine_kernel(own, faces, corners, child, face_idx, corner_idx, skip_grad, coarse_grad, total):
    bricks = own.shape[1]
    parents = coarse_grad.shape[1] // 8
    sel = one_hot(iota((2 * bricks, 64), 0) == face_idx[...])
    for g in range(32):
        got = jnp.concatenate([faces[e, g] for e in range(4)], 0)
        total[2 * g : 2 * g + 2] = own[2 * g : 2 * g + 2] + dot(sel, got).reshape(2, bricks, C)
    sel = one_hot(iota((8 * bricks, 64), 0) == corner_idx[...])
    for g in range(8):
        got = jnp.concatenate([corners[e, g] for e in range(4)], 0)
        new = total[8 * g : 8 * g + 8] + dot(sel, got).reshape(8, bricks, C)
        total[8 * g : 8 * g + 8] = new
        skip_grad[8 * g : 8 * g + 8] = new.astype(BF16)
    row = iota((8 * parents, bricks), 0)
    pick = one_hot((row % parents) * 8 + row // parents == child[...])
    for h in range(8):
        s = jnp.zeros((bricks, C), F32)
        for i in range(8):
            x, y, z = 2 * (h // 4) + i // 4, 2 * (h // 2 % 2) + i // 2 % 2, 2 * (h % 2) + i % 2
            s = s + total[16 * x + 4 * y + z]
        hi = s.astype(BF16)
        lo = (s - hi.astype(F32)).astype(BF16)
        coarse_grad[h] = (dot(pick, hi) + dot(pick, lo)).astype(BF16)


def call(kernel, outs, scratch, smem, *args):
    vm = pl.BlockSpec(memory_space=pltpu.VMEM)
    sm = pl.BlockSpec(memory_space=pltpu.SMEM)
    return pl.pallas_call(
        kernel,
        out_shape=[jax.ShapeDtypeStruct(s, d) for s, d in outs],
        in_specs=[sm if i in smem else vm for i in range(len(args))],
        out_specs=[vm] * len(outs),
        scratch_shapes=[pltpu.VMEM(s, d) for s, d in scratch],
        compiler_params=pltpu.CompilerParams(vmem_limit_bytes=40 * 1024 * 1024),
    )(*args)


def shift(value, step, n_x, n_y):
    route = []
    for i in range(n_x):
        for j in range(n_y):
            a, b = i + step[0], j + step[1]
            if 0 <= a < n_x and 0 <= b < n_y:
                route.append((i * n_y + j, a * n_y + b))
    return lax.ppermute(value, ("sx", "sy"), route)


def exchange(faces, corners, sign, n_x, n_y):
    moved = [
        shift(faces[k] if k < 4 else corners[k - 4], (sign * s[0], sign * s[1]), n_x, n_y)
        for k, s in enumerate(STEPS)
    ]
    return jnp.stack(moved[:4]), jnp.stack(moved[4:])


def local(n_x, n_y, skip_features, coarse_features, child_code, neighbours, send_face,
          send_corner, live_count, weight, conv_bias, cotangent):
    bricks = skip_features.shape[0]
    parents = coarse_features.shape[0]
    skip_t = skip_features.transpose(1, 0, 2)
    cot_t = cotangent.transpose(1, 0, 2)
    coarse_t = (
        coarse_features.reshape(parents, 2, 2, 2, 2, 2, 2, C)
        .transpose(2, 4, 6, 1, 3, 5, 0, 7)
        .reshape(8, 8 * parents, C)
    )
    face_idx = (send_face[0][:, None, :] + bricks * jnp.arange(2)[None, :, None]).reshape(-1)
    corner_idx = (send_corner[0][:, None, :] + bricks * jnp.arange(8)[None, :, None]).reshape(-1)
    nb = neighbours.T.reshape(-1, 1)
    pack_f, pack_c = ((4, 32, 16, C), BF16), ((4, 8, 16, C), BF16)
    hidden, faces, corners = call(
        hidden_kernel, [((64, bricks, C), BF16), pack_f, pack_c], [], (3,),
        skip_t, coarse_t, child_code[:, None], live_count, face_idx[:, None], corner_idx[:, None],
    )
    faces, corners = exchange(faces, corners, 1, n_x, n_y)
    act, grad, dwt, db = call(
        forward_kernel,
        [((64, bricks, C), BF16), ((64, bricks, C), BF16), ((C, 27 * C), F32), ((8, C), F32)],
        [((64, 80, C), BF16), ((6, 6, 6, 32, C), BF16), ((27 * 32, 80), BF16), ((512, 27 * C), BF16)],
        (4,),
        hidden, faces, corners, nb, live_count, weight.reshape(27 * C, C), conv_bias[None], cot_t,
    )
    dwt, db = lax.psum((dwt, jnp.sum(db, 0)), ("sx", "sy"))
    own, faces, corners = call(
        backward_kernel, [((64, bricks, C), F32), pack_f, pack_c],
        [((6, 6, 6, 32, C), F32), ((27 * 32, 80), BF16), ((64, 40, C), F32)], (),
        grad, nb, weight,
    )
    faces, corners = exchange(faces, corners, -1, n_x, n_y)
    skip_grad, coarse_grad = call(
        combine_kernel, [((64, bricks, C), BF16), ((8, 8 * parents, C), BF16)],
        [((64, bricks, C), F32)], (),
        own, faces, corners, child_code[None], face_idx[None], corner_idx[None],
    )
    coarse_grad = (
        coarse_grad.reshape(2, 2, 2, 2, 2, 2, parents, C)
        .transpose(6, 3, 0, 4, 1, 5, 2, 7)
        .reshape(parents, 64, C)
    )
    return (
        act.transpose(1, 0, 2),
        skip_grad.transpose(1, 0, 2),
        coarse_grad,
        dwt.reshape(C, 27, C).transpose(1, 2, 0),
        db,
    )


def solution(mesh):
    both = ("sx", "sy")
    three = P(both, None, None)
    return jax.shard_map(
        functools.partial(local, mesh.shape["sx"], mesh.shape["sy"]),
        mesh=mesh,
        in_specs=(three, three, P(both), P(both, None), three, three, P(both), P(), P(), three),
        out_specs=(three, three, three, P(), P()),
        check_vma=False,
    )
```

```python
import functools

import jax
import jax.numpy as jnp
from jax import lax
from jax.experimental import pallas as pl
from jax.experimental.pallas import tpu as pltpu
from jax.sharding import PartitionSpec as P

F32 = jnp.float32
BF16 = jnp.bfloat16
MESH = pl.DeviceIdType.MESH
C = 128
STEPS = ((1, 0), (-1, 0), (0, 1), (0, -1), (1, 1), (1, -1), (-1, 1), (-1, -1))


def sources():
    def along(s):
        out = [(1, s + 1)]
        if s == 0:
            out.append((2, 5))
        if s == 3:
            out.append((0, 0))
        return out

    table = {}
    for x in range(4):
        for y in range(4):
            for z in range(4):
                places = []
                for a, px in along(x):
                    for b, py in along(y):
                        for c, pz in along(z):
                            o = 9 * a + 3 * b + c
                            if o != 13:
                                places.append((o, px, py, pz))
                table[16 * x + 4 * y + z] = places
    return table


def iota(shape, dim):
    return lax.broadcasted_iota(jnp.int32, shape, dim)


def one_hot(cond):
    return cond.astype(F32).astype(BF16)


def dot(a, b, dims=((1,), (0,))):
    return lax.dot_general(a, b, (dims, ((), ())), preferred_element_type=F32)


def partners(sign, n_x, n_y):
    i, j = lax.axis_index("sx"), lax.axis_index("sy")

    def inside(a, b):
        return (a >= 0) & (a < n_x) & (b >= 0) & (b < n_y)

    return [
        (
            inside(i + sign * a, j + sign * b),
            inside(i - sign * a, j - sign * b),
            (jnp.clip(i + sign * a, 0, n_x - 1), jnp.clip(j + sign * b, 0, n_y - 1)),
        )
        for a, b in STEPS
    ]


def greet(sign, n_x, n_y):
    barrier = pltpu.get_barrier_semaphore()
    places = partners(sign, n_x, n_y)
    for out, _, target in places:
        @pl.when(out)
        def _():
            pl.semaphore_signal(barrier, inc=1, device_id=target, device_id_type=MESH)
    pl.semaphore_wait(barrier, sum(out.astype(jnp.int32) for out, _, _ in places))


def exchange(faces, corners, got_faces, got_corners, send_sem, recv_sem, sign, n_x, n_y):
    places = partners(sign, n_x, n_y)

    def copy(k):
        src, dst = (faces, got_faces) if k < 4 else (corners, got_corners)
        return pltpu.make_async_remote_copy(
            src_ref=src.at[k % 4], dst_ref=dst.at[k % 4], send_sem=send_sem.at[k],
            recv_sem=recv_sem.at[k], device_id=places[k][2], device_id_type=MESH)

    for k in range(8):
        @pl.when(places[k][0])
        def _():
            copy(k).start()
    for k in range(8):
        dst = got_faces if k < 4 else got_corners

        @pl.when(jnp.logical_not(places[k][1]))
        def _():
            dst[k % 4] = jnp.zeros_like(dst[k % 4])
    for k in range(8):
        @pl.when(places[k][1])
        def _():
            copy(k).wait_recv()
    for k in range(8):
        @pl.when(places[k][0])
        def _():
            copy(k).wait_send()


def hidden_kernel(n_x, n_y, skip, coarse, child, live, face_idx, corner_idx, hidden, got_faces,
                  got_corners, faces, corners, send_sem, recv_sem):
    greet(1, n_x, n_y)
    bricks = skip.shape[1]
    parents = coarse.shape[1] // 8
    col = iota((bricks, 8 * parents), 1)
    pick = one_hot(child[...] == (col % parents) * 8 + col // parents)
    keep = (iota((bricks, C), 0) < live[0]).astype(F32)
    for h in range(8):
        up = dot(pick, coarse[h])
        for i in range(8):
            x, y, z = 2 * (h // 4) + i // 4, 2 * (h // 2 % 2) + i // 2 % 2, 2 * (h % 2) + i % 2
            v = 16 * x + 4 * y + z
            hidden[v] = ((skip[v].astype(F32) + up) * keep).astype(BF16)
    sel = one_hot(face_idx[...] == iota((64, 2 * bricks), 1))
    for g in range(32):
        out = dot(sel, hidden[2 * g : 2 * g + 2].reshape(2 * bricks, C)).astype(BF16)
        for e in range(4):
            faces[e, g] = out[16 * e : 16 * e + 16]
    sel = one_hot(corner_idx[...] == iota((64, 8 * bricks), 1))
    for g in range(8):
        out = dot(sel, hidden[8 * g : 8 * g + 8].reshape(8 * bricks, C)).astype(BF16)
        for e in range(4):
            corners[e, g] = out[16 * e : 16 * e + 16]
    exchange(faces, corners, got_faces, got_corners, send_sem, recv_sem, 1, n_x, n_y)


def forward_kernel(hidden, faces, corners, nb, live, weight, bias, cot, act, grad, dwt,
                   table, pad, hot, cols):
    hot[...] = one_hot(nb[...] == iota(hot.shape, 1))
    table[:, 0:32] = hidden[...]
    for g in range(32):
        parts = [faces[e, g].astype(F32) for e in range(4)]
        for i in range(2):
            table[2 * g + i, 32:64] = jnp.concatenate(
                [p[8 * i : 8 * i + 8] for p in parts], 0).astype(BF16)
    row = iota((128, 64), 0)
    r = row % 16
    key = jnp.where(r < 8, (r // 2) * 16 + (row // 16) * 2 + r % 2, -1)
    spread = one_hot(key == iota((128, 64), 1))
    for g in range(8):
        got = jnp.concatenate([corners[e, g] for e in range(4)], 0)
        table[8 * g : 8 * g + 8, 64:80] = dot(spread, got).astype(BF16).reshape(8, 16, C)
    for x in range(4):
        pad[x + 1, 1:5, 1:5] = hidden[16 * x : 16 * x + 16].reshape(4, 4, 32, C)
    for v, places in sources().items():
        if places:
            stack = jnp.concatenate([hot[32 * o : 32 * o + 32] for o, *_ in places], 0)
            out = dot(stack, table[v]).astype(BF16)
            for i, (_, px, py, pz) in enumerate(places):
                pad[px, py, pz] = out[32 * i : 32 * i + 32]
    dwt[...] = jnp.zeros_like(dwt)
    cols[:, 27 * C :] = jnp.ones((512, C), BF16)
    keep = (iota((512, C), 0) % 32 < live[0]).astype(F32)

    def step(x, _):
        for t in range(27):
            tx, ty, tz = t // 9, t // 3 % 3, t % 3
            cols[:, C * t : C * t + C] = pad[x + tx, ty : ty + 4, tz : tz + 4].reshape(512, C)
        pre = dot(cols[:, : 27 * C], weight[...]) + bias[...]
        sg = 1.0 / (1.0 + jnp.exp(-pre))
        act[pl.ds(16 * x, 16)] = (pre * sg * keep).astype(BF16).reshape(16, 32, C)
        up = cot[pl.ds(16 * x, 16)].reshape(512, C).astype(F32)
        g = (up * sg * (1.0 + pre * (1.0 - sg)) * keep).astype(BF16)
        grad[pl.ds(16 * x, 16)] = g.reshape(16, 32, C)
        dwt[...] += dot(g.astype(F32).T.astype(BF16), cols[...])
        return 0

    lax.fori_loop(0, 4, step, 0)


def backward_kernel(grad, nb, weight, own, faces, corners, gp, hot, halo):
    hot[...] = one_hot(nb[...] == iota(hot.shape, 1))
    gp[...] = jnp.zeros_like(gp)

    def step(x, _):
        g = grad[pl.ds(16 * x, 16)].reshape(512, C)
        for t in range(27):
            tx, ty, tz = t // 9, t // 3 % 3, t % 3
            out = dot(g, weight[t], ((1,), (1,)))
            gp[x + tx, ty : ty + 4, tz : tz + 4] += out.reshape(4, 4, 32, C)
        return 0

    lax.fori_loop(0, 4, step, 0)
    for v, places in sources().items():
        mid = gp[v // 16 + 1, v // 4 % 4 + 1, v % 4 + 1]
        if places:
            stack = jnp.concatenate([hot[32 * o : 32 * o + 32] for o, *_ in places], 0)
            vals = jnp.concatenate([gp[a, b, c] for _, a, b, c in places], 0).astype(BF16)
            out = dot(stack, vals, ((0,), (0,)))
            own[v] = mid + out[0:32]
            halo[v] = out[32:72]
        else:
            own[v] = mid
            halo[v] = jnp.zeros((40, C), F32)
    for g in range(32):
        for e in range(4):
            faces[e, g] = halo[2 * g : 2 * g + 2, 8 * e : 8 * e + 8].reshape(16, C).astype(BF16)
    row = iota((64, 64), 0)
    key = (row % 16 // 2) * 8 + (row // 16) * 2 + row % 2
    pack = one_hot(key == iota((64, 64), 1))
    for g in range(8):
        part = halo[8 * g : 8 * g + 8, 32:40].reshape(64, C).astype(BF16)
        out = dot(pack, part).astype(BF16)
        for e in range(4):
            corners[e, g] = out[16 * e : 16 * e + 16]


def combine_kernel(n_x, n_y, own, sent_faces, sent_corners, child, face_idx, corner_idx, skip_grad,
                   coarse_grad, total, faces, corners, send_sem, recv_sem):
    greet(-1, n_x, n_y)
    exchange(sent_faces, sent_corners, faces, corners, send_sem, recv_sem, -1, n_x, n_y)
    bricks = own.shape[1]
    parents = coarse_grad.shape[1] // 8
    sel = one_hot(iota((2 * bricks, 64), 0) == face_idx[...])
    for g in range(32):
        got = jnp.concatenate([faces[e, g] for e in range(4)], 0)
        total[2 * g : 2 * g + 2] = own[2 * g : 2 * g + 2] + dot(sel, got).reshape(2, bricks, C)
    sel = one_hot(iota((8 * bricks, 64), 0) == corner_idx[...])
    for g in range(8):
        got = jnp.concatenate([corners[e, g] for e in range(4)], 0)
        new = total[8 * g : 8 * g + 8] + dot(sel, got).reshape(8, bricks, C)
        total[8 * g : 8 * g + 8] = new
        skip_grad[8 * g : 8 * g + 8] = new.astype(BF16)
    row = iota((8 * parents, bricks), 0)
    pick = one_hot((row % parents) * 8 + row // parents == child[...])
    for h in range(8):
        s = jnp.zeros((bricks, C), F32)
        for i in range(8):
            x, y, z = 2 * (h // 4) + i // 4, 2 * (h // 2 % 2) + i // 2 % 2, 2 * (h % 2) + i % 2
            s = s + total[16 * x + 4 * y + z]
        hi = s.astype(BF16)
        lo = (s - hi.astype(F32)).astype(BF16)
        coarse_grad[h] = (dot(pick, hi) + dot(pick, lo)).astype(BF16)


def call(kernel, outs, scratch, smem, *args, collective=None):
    vm = pl.BlockSpec(memory_space=pltpu.VMEM)
    sm = pl.BlockSpec(memory_space=pltpu.SMEM)
    sems = [] if collective is None else [pltpu.SemaphoreType.DMA((8,))] * 2
    return pl.pallas_call(
        kernel,
        out_shape=[jax.ShapeDtypeStruct(s, d) for s, d in outs],
        in_specs=[sm if i in smem else vm for i in range(len(args))],
        out_specs=[vm] * len(outs),
        scratch_shapes=[pltpu.VMEM(s, d) for s, d in scratch] + sems,
        compiler_params=pltpu.CompilerParams(
            vmem_limit_bytes=40 * 1024 * 1024,
            collective_id=collective,
            has_side_effects=collective is not None,
        ),
    )(*args)


def local(n_x, n_y, skip_features, coarse_features, child_code, neighbours, send_face,
          send_corner, live_count, weight, conv_bias, cotangent):
    bricks = skip_features.shape[0]
    parents = coarse_features.shape[0]
    skip_t = skip_features.transpose(1, 0, 2)
    cot_t = cotangent.transpose(1, 0, 2)
    coarse_t = (
        coarse_features.reshape(parents, 2, 2, 2, 2, 2, 2, C)
        .transpose(2, 4, 6, 1, 3, 5, 0, 7)
        .reshape(8, 8 * parents, C)
    )
    face_idx = (send_face[0][:, None, :] + bricks * jnp.arange(2)[None, :, None]).reshape(-1)
    corner_idx = (send_corner[0][:, None, :] + bricks * jnp.arange(8)[None, :, None]).reshape(-1)
    nb = neighbours.T.reshape(-1, 1)
    pack_f, pack_c = ((4, 32, 16, C), BF16), ((4, 8, 16, C), BF16)
    hidden, faces, corners = call(
        functools.partial(hidden_kernel, n_x, n_y),
        [((64, bricks, C), BF16), pack_f, pack_c], [pack_f, pack_c], (3,),
        skip_t, coarse_t, child_code[:, None], live_count, face_idx[:, None], corner_idx[:, None],
        collective=0,
    )
    act, grad, dwt = call(
        forward_kernel,
        [((64, bricks, C), BF16), ((64, bricks, C), BF16), ((C, 28 * C), F32)],
        [((64, 80, C), BF16), ((6, 6, 6, 32, C), BF16), ((27 * 32, 80), BF16), ((512, 28 * C), BF16)],
        (4,),
        hidden, faces, corners, nb, live_count, weight.reshape(27 * C, C), conv_bias[None], cot_t,
    )
    dwt = lax.psum(dwt, ("sx", "sy"))
    own, faces, corners = call(
        backward_kernel, [((64, bricks, C), F32), pack_f, pack_c],
        [((6, 6, 6, 32, C), F32), ((27 * 32, 80), BF16), ((64, 40, C), F32)], (),
        grad, nb, weight,
    )
    skip_grad, coarse_grad = call(
        functools.partial(combine_kernel, n_x, n_y),
        [((64, bricks, C), BF16), ((8, 8 * parents, C), BF16)],
        [((64, bricks, C), F32), pack_f, pack_c], (),
        own, faces, corners, child_code[None], face_idx[None], corner_idx[None],
        collective=1,
    )
    coarse_grad = (
        coarse_grad.reshape(2, 2, 2, 2, 2, 2, parents, C)
        .transpose(6, 3, 0, 4, 1, 5, 2, 7)
        .reshape(parents, 64, C)
    )
    return (
        act.transpose(1, 0, 2),
        skip_grad.transpose(1, 0, 2),
        coarse_grad,
        dwt[:, : 27 * C].reshape(C, 27, C).transpose(1, 2, 0),
        dwt[:, 27 * C],
    )


def solution(mesh):
    both = ("sx", "sy")
    three = P(both, None, None)
    return jax.shard_map(
        functools.partial(local, mesh.shape["sx"], mesh.shape["sy"]),
        mesh=mesh,
        in_specs=(three, three, P(both), P(both, None), three, three, P(both), P(), P(), three),
        out_specs=(three, three, three, P(), P()),
        check_vma=False,
    )
```

```python
import functools

import jax
import jax.numpy as jnp
from jax import lax
from jax.experimental import pallas as pl
from jax.experimental.pallas import tpu as pltpu
from jax.sharding import PartitionSpec as P

F32 = jnp.float32
BF16 = jnp.bfloat16
MESH = pl.DeviceIdType.MESH
C = 128
STEPS = ((1, 0), (-1, 0), (0, 1), (0, -1), (1, 1), (1, -1), (-1, 1), (-1, -1))


def sources():
    def along(s):
        out = [(1, s + 1)]
        if s == 0:
            out.append((2, 5))
        if s == 3:
            out.append((0, 0))
        return out

    table = {}
    for x in range(4):
        for y in range(4):
            for z in range(4):
                places = []
                for a, px in along(x):
                    for b, py in along(y):
                        for c, pz in along(z):
                            o = 9 * a + 3 * b + c
                            if o != 13:
                                places.append((o, px, py, pz))
                table[16 * x + 4 * y + z] = places
    return table


def iota(shape, dim):
    return lax.broadcasted_iota(jnp.int32, shape, dim)


def one_hot(cond):
    return cond.astype(F32).astype(BF16)


def dot(a, b, dims=((1,), (0,))):
    return lax.dot_general(a, b, (dims, ((), ())), preferred_element_type=F32)


def partners(sign, n_x, n_y):
    i, j = lax.axis_index("sx"), lax.axis_index("sy")

    def inside(a, b):
        return (a >= 0) & (a < n_x) & (b >= 0) & (b < n_y)

    return [
        (
            inside(i + sign * a, j + sign * b),
            inside(i - sign * a, j - sign * b),
            (jnp.clip(i + sign * a, 0, n_x - 1), jnp.clip(j + sign * b, 0, n_y - 1)),
        )
        for a, b in STEPS
    ]


def greet(sign, n_x, n_y):
    barrier = pltpu.get_barrier_semaphore()
    places = partners(sign, n_x, n_y)
    for out, _, target in places:
        @pl.when(out)
        def _():
            pl.semaphore_signal(barrier, inc=1, device_id=target, device_id_type=MESH)
    pl.semaphore_wait(barrier, sum(out.astype(jnp.int32) for out, _, _ in places))


def exchange(faces, corners, got_faces, got_corners, send_sem, recv_sem, sign, n_x, n_y):
    places = partners(sign, n_x, n_y)

    def copy(k):
        src, dst = (faces, got_faces) if k < 4 else (corners, got_corners)
        return pltpu.make_async_remote_copy(
            src_ref=src.at[k % 4], dst_ref=dst.at[k % 4], send_sem=send_sem.at[k],
            recv_sem=recv_sem.at[k], device_id=places[k][2], device_id_type=MESH)

    for k in range(8):
        @pl.when(places[k][0])
        def _():
            copy(k).start()
    for k in range(8):
        dst = got_faces if k < 4 else got_corners

        @pl.when(jnp.logical_not(places[k][1]))
        def _():
            dst[k % 4] = jnp.zeros_like(dst[k % 4])
    for k in range(8):
        @pl.when(places[k][1])
        def _():
            copy(k).wait_recv()
    for k in range(8):
        @pl.when(places[k][0])
        def _():
            copy(k).wait_send()


def hidden_kernel(n_x, n_y, skip, coarse, child, live, face_idx, corner_idx, hidden, got_faces,
                  got_corners, faces, corners, send_sem, recv_sem):
    greet(1, n_x, n_y)
    bricks = skip.shape[1]
    parents = coarse.shape[1] // 8
    col = iota((bricks, 8 * parents), 1)
    pick = one_hot(child[...] == (col % parents) * 8 + col // parents)
    keep = (iota((bricks, C), 0) < live[0]).astype(F32)
    for h in range(8):
        up = dot(pick, coarse[h])
        for i in range(8):
            x, y, z = 2 * (h // 4) + i // 4, 2 * (h // 2 % 2) + i // 2 % 2, 2 * (h % 2) + i % 2
            v = 16 * x + 4 * y + z
            hidden[v] = ((skip[v].astype(F32) + up) * keep).astype(BF16)
    sel = one_hot(face_idx[...] == iota((64, 2 * bricks), 1))
    for g in range(32):
        out = dot(sel, hidden[2 * g : 2 * g + 2].reshape(2 * bricks, C)).astype(BF16)
        for e in range(4):
            faces[e, g] = out[16 * e : 16 * e + 16]
    sel = one_hot(corner_idx[...] == iota((64, 8 * bricks), 1))
    for g in range(8):
        out = dot(sel, hidden[8 * g : 8 * g + 8].reshape(8 * bricks, C)).astype(BF16)
        for e in range(4):
            corners[e, g] = out[16 * e : 16 * e + 16]
    exchange(faces, corners, got_faces, got_corners, send_sem, recv_sem, 1, n_x, n_y)


def forward_kernel(hidden, faces, corners, nb, live, weight, bias, cot, act, grad, dwt,
                   table, pad, hot, cols):
    hot[...] = one_hot(nb[...] == iota(hot.shape, 1))
    table[:, 0:32] = hidden[...]
    for g in range(32):
        parts = [faces[e, g].astype(F32) for e in range(4)]
        for i in range(2):
            table[2 * g + i, 32:64] = jnp.concatenate(
                [p[8 * i : 8 * i + 8] for p in parts], 0).astype(BF16)
    row = iota((128, 64), 0)
    r = row % 16
    key = jnp.where(r < 8, (r // 2) * 16 + (row // 16) * 2 + r % 2, -1)
    spread = one_hot(key == iota((128, 64), 1))
    for g in range(8):
        got = jnp.concatenate([corners[e, g] for e in range(4)], 0)
        table[8 * g : 8 * g + 8, 64:80] = dot(spread, got).astype(BF16).reshape(8, 16, C)
    for x in range(4):
        pad[x + 1, 1:5, 1:5] = hidden[16 * x : 16 * x + 16].reshape(4, 4, 32, C)
    for v, places in sources().items():
        if places:
            stack = jnp.concatenate([hot[32 * o : 32 * o + 32] for o, *_ in places], 0)
            out = dot(stack, table[v]).astype(BF16)
            for i, (_, px, py, pz) in enumerate(places):
                pad[px, py, pz] = out[32 * i : 32 * i + 32]
    dwt[...] = jnp.zeros_like(dwt)
    cols[:, 27 * C :] = jnp.ones((512, C), BF16)
    keep = (iota((512, C), 0) % 32 < live[0]).astype(F32)

    def step(x, _):
        for t in range(27):
            tx, ty, tz = t // 9, t // 3 % 3, t % 3
            cols[:, C * t : C * t + C] = pad[x + tx, ty : ty + 4, tz : tz + 4].reshape(512, C)
        pre = dot(cols[:, : 27 * C], weight[...]) + bias[...]
        sg = 1.0 / (1.0 + jnp.exp(-pre))
        act[pl.ds(16 * x, 16)] = (pre * sg * keep).astype(BF16).reshape(16, 32, C)
        up = cot[pl.ds(16 * x, 16)].reshape(512, C).astype(F32)
        g = (up * sg * (1.0 + pre * (1.0 - sg)) * keep).astype(BF16)
        grad[pl.ds(16 * x, 16)] = g.reshape(16, 32, C)
        term = dot(g.astype(F32).T.astype(BF16), cols[...])
        for t in range(28):
            dwt[C * t : C * t + C] += term[:, C * t : C * t + C]
        return 0

    lax.fori_loop(0, 4, step, 0)


def backward_kernel(grad, nb, weight, own, faces, corners, gp, hot, halo):
    hot[...] = one_hot(nb[...] == iota(hot.shape, 1))
    gp[...] = jnp.zeros_like(gp)

    def step(x, _):
        g = grad[pl.ds(16 * x, 16)].reshape(512, C)
        for t in range(27):
            tx, ty, tz = t // 9, t // 3 % 3, t % 3
            out = dot(g, weight[t], ((1,), (1,)))
            gp[x + tx, ty : ty + 4, tz : tz + 4] += out.reshape(4, 4, 32, C)
        return 0

    lax.fori_loop(0, 4, step, 0)
    for v, places in sources().items():
        mid = gp[v // 16 + 1, v // 4 % 4 + 1, v % 4 + 1]
        if places:
            stack = jnp.concatenate([hot[32 * o : 32 * o + 32] for o, *_ in places], 0)
            vals = jnp.concatenate([gp[a, b, c] for _, a, b, c in places], 0).astype(BF16)
            out = dot(stack, vals, ((0,), (0,)))
            own[v] = mid + out[0:32]
            halo[v] = out[32:72]
        else:
            own[v] = mid
            halo[v] = jnp.zeros((40, C), F32)
    for g in range(32):
        for e in range(4):
            faces[e, g] = halo[2 * g : 2 * g + 2, 8 * e : 8 * e + 8].reshape(16, C).astype(BF16)
    row = iota((64, 64), 0)
    key = (row % 16 // 2) * 8 + (row // 16) * 2 + row % 2
    pack = one_hot(key == iota((64, 64), 1))
    for g in range(8):
        part = halo[8 * g : 8 * g + 8, 32:40].reshape(64, C).astype(BF16)
        out = dot(pack, part).astype(BF16)
        for e in range(4):
            corners[e, g] = out[16 * e : 16 * e + 16]


def combine_kernel(n_x, n_y, own, sent_faces, sent_corners, child, face_idx, corner_idx, skip_grad,
                   coarse_grad, total, faces, corners, send_sem, recv_sem):
    greet(-1, n_x, n_y)
    exchange(sent_faces, sent_corners, faces, corners, send_sem, recv_sem, -1, n_x, n_y)
    bricks = own.shape[1]
    parents = coarse_grad.shape[1] // 8
    sel = one_hot(iota((2 * bricks, 64), 0) == face_idx[...])
    for g in range(32):
        got = jnp.concatenate([faces[e, g] for e in range(4)], 0)
        total[2 * g : 2 * g + 2] = own[2 * g : 2 * g + 2] + dot(sel, got).reshape(2, bricks, C)
    sel = one_hot(iota((8 * bricks, 64), 0) == corner_idx[...])
    for g in range(8):
        got = jnp.concatenate([corners[e, g] for e in range(4)], 0)
        new = total[8 * g : 8 * g + 8] + dot(sel, got).reshape(8, bricks, C)
        total[8 * g : 8 * g + 8] = new
        skip_grad[8 * g : 8 * g + 8] = new.astype(BF16)
    row = iota((8 * parents, bricks), 0)
    pick = one_hot((row % parents) * 8 + row // parents == child[...])
    for h in range(8):
        s = jnp.zeros((bricks, C), F32)
        for i in range(8):
            x, y, z = 2 * (h // 4) + i // 4, 2 * (h // 2 % 2) + i // 2 % 2, 2 * (h % 2) + i % 2
            s = s + total[16 * x + 4 * y + z]
        hi = s.astype(BF16)
        lo = (s - hi.astype(F32)).astype(BF16)
        coarse_grad[h] = (dot(pick, hi) + dot(pick, lo)).astype(BF16)


def sum_kernel(n_x, n_y, term, weight_grad, bias_grad, sent, got, held, onward, arrived, result,
               send_sem, recv_sem):
    i, j = lax.axis_index("sx"), lax.axis_index("sy")
    part, piece = onward.shape[0], arrived.shape[1]
    x_peers = [lax.rem(i + d, n_x) for d in range(1, n_x)]
    y_peers = [lax.rem(j + d, n_y) for d in range(1, n_y)]
    devices = [(p, j) for p in x_peers] + [(i, q) for q in y_peers]
    barrier = pltpu.get_barrier_semaphore()
    for device in devices:
        pl.semaphore_signal(barrier, inc=1, device_id=device, device_id_type=MESH)
    sent[...] = term[...].astype(BF16)
    pl.semaphore_wait(barrier, len(devices))

    def rows(start, size):
        return pl.ds(pl.multiple_of(start, 16), size)

    def copy(k, src, dst, device):
        return pltpu.make_async_remote_copy(
            src_ref=src, dst_ref=dst, send_sem=send_sem.at[k], recv_sem=recv_sem.at[k],
            device_id=device, device_id_type=MESH)

    def run(copies):
        for c in copies:
            c.start()
        for c in copies:
            c.wait_recv()
        return copies

    nx, ny = n_x - 1, n_y - 1
    own_x, own_y = rows(i * part, part), rows(j * piece, piece)
    first = run([copy(d, sent.at[rows(p * part, part)], got.at[d], (p, j))
                 for d, p in enumerate(x_peers)])
    total = term[own_x]
    for d in range(nx):
        total = total + got[d].astype(F32)
    held[...] = total
    onward[...] = total.astype(BF16)
    second = run([copy(nx + d, onward.at[rows(q * piece, piece)], arrived.at[d], (i, q))
                  for d, q in enumerate(y_peers)])
    total = held[own_y]
    for d in range(ny):
        total = total + arrived[d].astype(F32)
    mine = rows(i * part + j * piece, piece)
    result[mine] = total.astype(BF16)
    third = run([copy(nx + ny + d, result.at[mine], result.at[mine], (i, q))
                 for d, q in enumerate(y_peers)])
    fourth = run([copy(nx + 2 * ny + d, result.at[own_x], result.at[own_x], (p, j))
                  for d, p in enumerate(x_peers)])
    for t in range(27):
        weight_grad[t] = result[C * t : C * t + C].astype(F32).T
    bias_grad[...] = result[27 * C : 28 * C].astype(F32).T[0:8]
    for c in first + second + third + fourth:
        c.wait_send()


def call(kernel, outs, scratch, smem, *args, collective=None, n_sems=8):
    vm = pl.BlockSpec(memory_space=pltpu.VMEM)
    sm = pl.BlockSpec(memory_space=pltpu.SMEM)
    sems = [] if collective is None else [pltpu.SemaphoreType.DMA((n_sems,))] * 2
    return pl.pallas_call(
        kernel,
        out_shape=[jax.ShapeDtypeStruct(s, d) for s, d in outs],
        in_specs=[sm if i in smem else vm for i in range(len(args))],
        out_specs=[vm] * len(outs),
        scratch_shapes=[pltpu.VMEM(s, d) for s, d in scratch] + sems,
        compiler_params=pltpu.CompilerParams(
            vmem_limit_bytes=40 * 1024 * 1024,
            collective_id=collective,
            has_side_effects=collective is not None,
        ),
    )(*args)


def local(n_x, n_y, skip_features, coarse_features, child_code, neighbours, send_face,
          send_corner, live_count, weight, conv_bias, cotangent):
    bricks = skip_features.shape[0]
    parents = coarse_features.shape[0]
    skip_t = skip_features.transpose(1, 0, 2)
    cot_t = cotangent.transpose(1, 0, 2)
    coarse_t = (
        coarse_features.reshape(parents, 2, 2, 2, 2, 2, 2, C)
        .transpose(2, 4, 6, 1, 3, 5, 0, 7)
        .reshape(8, 8 * parents, C)
    )
    face_idx = (send_face[0][:, None, :] + bricks * jnp.arange(2)[None, :, None]).reshape(-1)
    corner_idx = (send_corner[0][:, None, :] + bricks * jnp.arange(8)[None, :, None]).reshape(-1)
    nb = neighbours.T.reshape(-1, 1)
    pack_f, pack_c = ((4, 32, 16, C), BF16), ((4, 8, 16, C), BF16)
    hidden, faces, corners = call(
        functools.partial(hidden_kernel, n_x, n_y),
        [((64, bricks, C), BF16), pack_f, pack_c], [pack_f, pack_c], (3,),
        skip_t, coarse_t, child_code[:, None], live_count, face_idx[:, None], corner_idx[:, None],
        collective=0,
    )
    act, grad, dwt = call(
        forward_kernel,
        [((64, bricks, C), BF16), ((64, bricks, C), BF16), ((28 * C, C), F32)],
        [((64, 80, C), BF16), ((6, 6, 6, 32, C), BF16), ((27 * 32, 80), BF16), ((512, 28 * C), BF16)],
        (4,),
        hidden, faces, corners, nb, live_count, weight.reshape(27 * C, C), conv_bias[None], cot_t,
    )
    unit = 16 * n_x * n_y
    rows = -(-28 * C // unit) * unit
    dwt = jnp.pad(dwt, ((0, rows - 28 * C), (0, 0)))
    own, faces, corners = call(
        backward_kernel, [((64, bricks, C), F32), pack_f, pack_c],
        [((6, 6, 6, 32, C), F32), ((27 * 32, 80), BF16), ((64, 40, C), F32)], (),
        grad, nb, weight,
    )
    skip_grad, coarse_grad = call(
        functools.partial(combine_kernel, n_x, n_y),
        [((64, bricks, C), BF16), ((8, 8 * parents, C), BF16)],
        [((64, bricks, C), F32), pack_f, pack_c], (),
        own, faces, corners, child_code[None], face_idx[None], corner_idx[None],
        collective=1,
    )
    part, piece = rows // n_x, rows // (n_x * n_y)
    weight_grad, bias_grad = call(
        functools.partial(sum_kernel, n_x, n_y),
        [((27, C, C), F32), ((8, C), F32)],
        [((rows, C), BF16), ((n_x - 1, part, C), BF16), ((part, C), F32), ((part, C), BF16),
         ((n_y - 1, piece, C), BF16), ((rows, C), BF16)],
        (), dwt, collective=2, n_sems=2 * (n_x + n_y - 2),
    )
    coarse_grad = (
        coarse_grad.reshape(2, 2, 2, 2, 2, 2, parents, C)
        .transpose(6, 3, 0, 4, 1, 5, 2, 7)
        .reshape(parents, 64, C)
    )
    return (
        act.transpose(1, 0, 2),
        skip_grad.transpose(1, 0, 2),
        coarse_grad,
        weight_grad,
        bias_grad[0],
    )


def solution(mesh):
    both = ("sx", "sy")
    three = P(both, None, None)
    return jax.shard_map(
        functools.partial(local, mesh.shape["sx"], mesh.shape["sy"]),
        mesh=mesh,
        in_specs=(three, three, P(both), P(both, None), three, three, P(both), P(), P(), three),
        out_specs=(three, three, three, P(), P()),
        check_vma=False,
    )
```
